512 devices in a mesh: row: 16 (over y, x_hi), col: 32 (over z, x_lo, core).
Axes of the slice: x: 4 (x_hi: 2, x_lo: 2; x = x_hi * 2 + x_lo), y: 8, z: 8, core: 2. Of those that a mesh axis runs over, the one named last changes fastest.
Arguments:
- matrix: float32 [12288, 12288], P('row', 'col'), may hold values from -24 to 24
- vectors: float32 [12288, 12288], P('row', 'col'), may hold values from -6 to 6
- rotations: float32 [16, 768, 768], P('row', 'col'), may hold values from -0.21875 to 0.21875
Outputs:
- new_matrix: float32 [12288, 12288], P('row', 'col')
- new_vectors: float32 [12288, 12288], P('row', 'col')
The draws below stay inside these ranges and needn't reach their ends.
All inputs are finite; a program needn't handle non-finite values.
Results may differ from the reference program's by a relative error of at most 0.000096.
Values sent between devices are 32-bit elements; how exact they have to be, the bound alone decides.
A program may use at most 64 MiB of HBM per device.

```python
import jax
import jax.numpy as jnp
import numpy as np
from jax import lax

B = 384
PAIRS = 16
ORDER = 12288
N_ROW = 16


def draw_matrix(key, part):
    key = jax.random.fold_in(key, 5)
    base = jax.random.truncated_normal(key, -6.0, 6.0, (ORDER, ORDER), jnp.float32)
    return (base + base.T) * 0.70710678


def levels(own_key, shape, pieces, smallest, largest):
    def one(position, shards_of):
        draws = jax.random.uniform(jax.random.fold_in(jax.random.fold_in(own_key, 6), position), (shards_of,), jnp.float32, smallest / len(pieces), largest / len(pieces))
        return jnp.repeat(jnp.exp(draws), shape[position] // shards_of).reshape((-1,) + (1,) * (len(shape) - position - 1))

    gain = one(*pieces[0])
    for cut in pieces[1:]:
        gain = gain * one(*cut)
    return gain


def centred(rng, dims, scale, bound, pieces=(), kind=jnp.bfloat16):
    level = levels(rng, dims, pieces, -0.22, 0.18) if pieces else 1.0
    entries = jax.random.normal(rng, dims, jnp.float32) * scale * level
    return jnp.minimum(jnp.maximum(entries, -bound), bound).astype(kind)


def setup_inputs(seed: int = 0) -> dict:
    seeds = jax.random.split(jax.random.key(seed), 4)
    return {
        "matrix": draw_matrix(jax.random.fold_in(seeds[3], 71), 0),
        "vectors": centred(seeds[1], (ORDER, ORDER), 1.0, 6.0, ((0, 16), (1, 32)), jnp.float32),
        "rotations": centred(seeds[2], (PAIRS, 2 * B, 2 * B), (2 * B) ** -0.5, 0.21875, ((0, 16), (1, 32)), jnp.float32),
    }


def source_blocks(count):
    table = []
    for k in range(count):
        if k == 0:
            table.append(0)
        elif k == 2:
            table.append(1)
        elif k == count - 1:
            table.append(count - 2)
        elif k % 2 == 0:
            table.append(k - 2)
        else:
            table.append(k + 2)
    return np.array(table, dtype=np.int32)


def reference(matrix, vectors, rotations):
    pairs = N_ROW
    width = B
    order = matrix.shape[0]
    high = lax.Precision.HIGHEST
    stacked = matrix.reshape(pairs, 2 * width, order)
    left = jnp.einsum('pkb,pkn->pbn', rotations, stacked, precision=high).reshape(order, order)

    def right_side(field):
        shaped = field.reshape(order, pairs, 2 * width)
        return jnp.einsum('mpk,pkb->mpb', shaped, rotations, precision=high).reshape(order, order)

    rotated = right_side(left)
    turned = right_side(vectors)
    source = jnp.asarray(source_blocks(2 * pairs))
    blocks = rotated.reshape(2 * pairs, width, 2 * pairs, width)
    blocks = jnp.take(jnp.take(blocks, source, axis=0), source, axis=2)
    new_matrix = blocks.reshape(order, order)
    new_vectors = jnp.take(turned.reshape(order, 2 * pairs, width), source, axis=1).reshape(order, order)
    return new_matrix, new_vectors
```

```python
import functools

import jax
import jax.numpy as jnp
from jax import lax
from jax.experimental import pallas as pl
from jax.experimental.pallas import tpu as pltpu
from jax.sharding import PartitionSpec as P

MESH = pl.DeviceIdType.MESH
F32 = jnp.float32
BF16 = jnp.bfloat16


def target(k, count):
    moved = jnp.where(lax.rem(k, 2) == 0, k + 2, k - 2)
    moved = jnp.where(k == count - 2, count - 1, moved)
    moved = jnp.where(k == 1, 2, moved)
    return jnp.where(k == 0, 0, moved)


def origin(k, count):
    moved = jnp.where(lax.rem(k, 2) == 0, k - 2, k + 2)
    moved = jnp.where(k == count - 1, count - 2, moved)
    moved = jnp.where(k == 2, 1, moved)
    return jnp.where(k == 0, 0, moved)


def halves(value):
    high = value.astype(BF16)
    return high, (value - high.astype(F32)).astype(BF16)


def product(a, b, contract):
    dims = ((contract, (0,)), ((), ()))
    dot = functools.partial(lax.dot_general, dimension_numbers=dims, preferred_element_type=F32)
    return dot(a[0], b[0]) + (dot(a[0], b[1]) + dot(a[1], b[0]))


def kernel(n_row, n_col, m_ref, v_ref, rot_ref, om_ref, ov_ref, mf, vf, rp, rr, rph, rpl, mrh, mrl,
           out_v, out_m, send_sem, recv_sem, loc_sem):
    height, width = m_ref.shape
    full = 2 * width
    shard = rot_ref.shape[1]
    n_y, n_z = n_row // 2, n_col // 4
    r, c = lax.axis_index("row"), lax.axis_index("col")
    y, h = lax.div(r, 2), lax.rem(r, 2)
    p, s = lax.div(c, 2), lax.rem(c, 2)
    z, l = lax.div(p, 2), lax.rem(p, 2)
    core, lane = (r, c + 1 - 2 * s), (r, c + 2 - 4 * l)
    z_next, z_last = (r, lax.rem(c + 4, n_col)), (r, lax.rem(c + n_col - 4, n_col))
    half_row = (r + 1 - 2 * h, c)
    y_next, y_last = (lax.rem(r + 2, n_row), c), (lax.rem(r + n_row - 2, n_row), c)
    across = [(p, 2 * r + t) for t in range(2)]
    across_self = [(p == r) & (s == t) for t in range(2)]
    col_to, col_from = target(c, n_col), origin(c, n_col)
    row_to = [target(2 * r + u, 2 * n_row) for u in range(2)]
    row_from = [origin(2 * r + u, 2 * n_row) for u in range(2)]
    v_to, v_from = (r, col_to), (r, col_from)
    v_self = col_to == c
    m_to = [(lax.div(row_to[u], 2), col_to) for u in range(2)]
    m_from = [(lax.div(row_from[u], 2), col_from) for u in range(2)]
    m_self = [(m_to[u][0] == r) & (col_to == c) for u in range(2)]
    m_same = [(m_from[u][0] == r) & (col_from == c) for u in range(2)]

    barrier = pltpu.get_barrier_semaphore()
    awaited = 7

    def greet(device):
        pl.semaphore_signal(barrier, inc=1, device_id=device, device_id_type=MESH)

    for device in (core, lane, z_next, z_last, half_row, y_next, y_last):
        greet(device)
    for same in (*across_self, v_self, *m_self):
        awaited = awaited + jnp.where(same, 0, 1)
    for device, same in ((across[0], across_self[0]), (across[1], across_self[1]), (v_from, v_self),
                         (m_from[0], m_same[0]), (m_from[1], m_same[1])):
        pl.when(jnp.logical_not(same))(functools.partial(greet, device))

    own = pltpu.make_async_copy(rot_ref.at[0], rr.at[z, l, s], loc_sem.at[0])
    own.start()
    own_m = pltpu.make_async_copy(m_ref, mf.at[:, pl.ds(pl.multiple_of(s * width, width), width)], loc_sem.at[1])
    own_v = pltpu.make_async_copy(v_ref, vf.at[:, pl.ds(pl.multiple_of(s * width, width), width)], loc_sem.at[2])
    own_m.start()
    own_v.start()
    pl.semaphore_wait(barrier, awaited)

    index = iter(range(200))
    sends = []

    def describe(src, dst, device, sem=None):
        sem = next(index) if sem is None else sem
        return pltpu.make_async_remote_copy(
            src_ref=src, dst_ref=dst, send_sem=send_sem.at[sem], recv_sem=recv_sem.at[sem],
            device_id=device, device_id_type=MESH)

    def send(src, dst, device):
        copy = describe(src, dst, device)
        copy.start()
        sends.append(copy)
        return copy

    crossed = []
    for t in range(2):
        src = rot_ref.at[0, :, t * width:(t + 1) * width]
        sem = next(index)
        far = describe(src, rp.at[c], across[t], sem)
        near = pltpu.make_async_copy(src, rp.at[c], recv_sem.at[sem])
        pl.when(jnp.logical_not(across_self[t]))(far.start)
        pl.when(across_self[t])(near.start)
        crossed.append((far, across_self[t], t, sem))
    src = rot_ref.at[0]
    ring_z = {(0, 1, 0): send(src, rr.at[z, l, s], z_next), (0, -1, 0): send(src, rr.at[z, l, s], z_last)}
    to_lane = send(src, rr.at[z, l, s], lane)
    mine = pl.ds(pl.multiple_of(s * width, width), width)
    got_v = send(v_ref, vf.at[:, mine], core)
    got_m = send(m_ref, mf.at[:, mine], core)

    def row_block(who_y, who_h):
        return rp.at[pl.ds(2 * (2 * who_y + who_h), 2)]

    def chip_block(who_z, who_l):
        return rr.at[who_z, who_l, s]

    for t in range(2):
        far, _, _, sem = crossed[t]
        pl.when(s == t)(lambda sem=sem: pltpu.make_async_copy(
            rp.at[pl.ds(2 * r, 2)], rp.at[pl.ds(2 * r, 2)], recv_sem.at[sem]).wait())
    block = row_block(y, h)
    ring_y = {(0, 1, 0): send(block, block, y_next), (0, -1, 0): send(block, block, y_last)}
    to_half = send(block, block, half_row)

    to_lane.wait_recv()
    for d, device in ((1, z_next), (-1, z_last)):
        ring_z[0, d, 1] = send(chip_block(z, 1 - l), chip_block(z, 1 - l), device)
    own.wait()
    both = rr.at[z, :, s]
    core_z = [send(both, both, core)]
    to_half.wait_recv()
    block = row_block(y, 1 - h)
    for d, device in ((1, y_next), (-1, y_last)):
        ring_y[0, d, 1] = send(block, block, device)

    def ring(k, size, ring_of, place, pick, ways):
        far = size // 2
        for lane_of in range(2):
            for d, device in ways:
                if (k - 1, d, lane_of) not in ring_of:
                    continue
                ring_of[k - 1, d, lane_of].wait_recv()
                at = lax.rem(place - d * k + size, size)
                block = pick(at, lane_of)
                if k < far - 1 or (k == far - 1 and (d == 1) == (lane_of == 0)):
                    ring_of[k, d, lane_of] = send(block, block, device)

    pick_y = lambda at, lane_of: row_block(at, h if lane_of == 0 else 1 - h)
    pick_z = lambda at, lane_of: chip_block(at, l if lane_of == 0 else 1 - l)
    ways_y, ways_z = ((1, y_next), (-1, y_last)), ((1, z_next), (-1, z_last))
    for k in range(1, max(n_y, n_z) // 2 + 1):
        if k <= n_y // 2:
            ring(k, n_y, ring_y, y, pick_y, ways_y)
        if k <= n_z // 2:
            ring(k, n_z, ring_z, z, pick_z, ways_z)
            for d in (1, -1) if k < n_z // 2 else (1,):
                both = rr.at[lax.rem(z - d * k + n_z, n_z), :, s]
                core_z.append(send(both, both, core))
    own_v.wait()
    own_m.wait()
    got_v.wait_recv()
    got_m.wait_recv()

    count = n_col // 4
    rows_of = 4 * shard

    @pl.loop(0, count)
    def _(i):
        high, low = halves(rp[pl.ds(4 * i, 4)].reshape(rows_of, width))
        at = pl.ds(pl.multiple_of(i * rows_of, rows_of), rows_of)
        rph[at, :] = high
        rpl[at, :] = low

    step = 256 if height % 256 == 0 else height // 3
    v_sem = next(index)
    m_sem = [next(index) for _ in range(2)]

    def move(src, dst, device, same, sem):
        far = describe(src, dst, device, sem)
        pl.when(jnp.logical_not(same))(far.start)
        pl.when(same)(pltpu.make_async_copy(src, dst, recv_sem.at[sem]).start)

    @pl.loop(0, height // step)
    def _(i):
        at = pl.ds(pl.multiple_of(i * step, step), step)
        out_v[at, :] = product(halves(vf[at, :]), (rph[...], rpl[...]), (1,))
        move(out_v.at[at], ov_ref.at[at], v_to, v_self, v_sem)

    @pl.loop(0, height // step)
    def _(i):
        at = pl.ds(pl.multiple_of(i * step, step), step)
        high, low = halves(product(halves(mf[at, :]), (rph[...], rpl[...]), (1,)))
        mrh[at, :] = high
        mrl[at, :] = low

    for copy in core_z:
        copy.wait_recv()

    tile = 128 if width % 128 == 0 else width
    for u in range(2):
        slot = lax.rem(row_to[u], 2)
        dst_base = slot * width
        sem = jnp.where(slot == 0, m_sem[0], m_sem[1])

        @pl.loop(0, width // tile)
        def _(i):
            src_at = pl.multiple_of(u * width + i * tile, tile)
            part = rr[:, :, :, :, pl.ds(src_at, tile)].reshape(height, tile)
            at = pl.ds(src_at, tile)
            out_m[at, :] = product(halves(part), (mrh[...], mrl[...]), (0,))
            to = pl.ds(pl.multiple_of(dst_base + i * tile, tile), tile)
            move(out_m.at[at], om_ref.at[to], m_to[u], m_self[u], sem)

    pltpu.make_async_copy(ov_ref, ov_ref, recv_sem.at[v_sem]).wait()
    for u in range(2):
        part = om_ref.at[u * width:(u + 1) * width]
        pltpu.make_async_copy(part, part, recv_sem.at[m_sem[u]]).wait()
    for copy in sends:
        copy.wait_send()
    for far, same, _, _ in crossed:
        pl.when(jnp.logical_not(same))(far.wait_send)
    v_out = describe(out_v, ov_ref, v_to, v_sem)
    pl.when(jnp.logical_not(v_self))(v_out.wait_send)
    for u in range(2):
        slot = lax.rem(row_to[u], 2)
        sem = jnp.where(slot == 0, m_sem[0], m_sem[1])
        part = out_m.at[u * width:(u + 1) * width]
        out = describe(part, om_ref.at[0:width], m_to[u], sem)
        pl.when(jnp.logical_not(m_self[u]))(out.wait_send)


def solution(mesh):
    n_row, n_col = mesh.shape["row"], mesh.shape["col"]

    def on_device(matrix, vectors, rotations):
        height, width = matrix.shape
        shard = rotations.shape[1]
        any_space = pl.BlockSpec(memory_space=pl.ANY)
        return pl.pallas_call(
            functools.partial(kernel, n_row, n_col),
            out_shape=[jax.ShapeDtypeStruct((height, width), F32)] * 2,
            in_specs=[any_space] * 3,
            out_specs=[any_space] * 2,
            scratch_shapes=[
                pltpu.VMEM((height, 2 * width), F32),
                pltpu.VMEM((height, 2 * width), F32),
                pltpu.VMEM((n_col, shard, width), F32),
                pltpu.VMEM((n_col // 4, 2, 2, shard, 2 * width), F32),
                pltpu.VMEM((height, width), BF16),
                pltpu.VMEM((height, width), BF16),
                pltpu.VMEM((height, width), BF16),
                pltpu.VMEM((height, width), BF16),
                pltpu.VMEM((height, width), F32),
                pltpu.VMEM((height, width), F32),
                pltpu.SemaphoreType.DMA((64,)),
                pltpu.SemaphoreType.DMA((64,)),
                pltpu.SemaphoreType.DMA((3,)),
            ],
            compiler_params=pltpu.CompilerParams(
                collective_id=0, has_side_effects=True, vmem_limit_bytes=40 * 1024 * 1024),
            name="round",
        )(matrix, vectors, rotations)

    return jax.shard_map(
        on_device, mesh=mesh,
        in_specs=(P("row", "col"), P("row", "col"), P("row", "col", None)),
        out_specs=(P("row", "col"), P("row", "col")), check_vma=False)
```

```python
import functools

import jax
import jax.numpy as jnp
from jax import lax
from jax.experimental import pallas as pl
from jax.experimental.pallas import tpu as pltpu
from jax.sharding import PartitionSpec as P

MESH = pl.DeviceIdType.MESH
F32 = jnp.float32
BF16 = jnp.bfloat16


def target(k, count):
    moved = jnp.where(lax.rem(k, 2) == 0, k + 2, k - 2)
    moved = jnp.where(k == count - 2, count - 1, moved)
    moved = jnp.where(k == 1, 2, moved)
    return jnp.where(k == 0, 0, moved)


def origin(k, count):
    moved = jnp.where(lax.rem(k, 2) == 0, k - 2, k + 2)
    moved = jnp.where(k == count - 1, count - 2, moved)
    moved = jnp.where(k == 2, 1, moved)
    return jnp.where(k == 0, 0, moved)


def halves(value):
    high = value.astype(BF16)
    return high, (value - high.astype(F32)).astype(BF16)


def product(a, b, contract):
    dims = ((contract, (0,)), ((), ()))
    dot = functools.partial(lax.dot_general, dimension_numbers=dims, preferred_element_type=F32)
    return dot(a[0], b[0]) + (dot(a[0], b[1]) + dot(a[1], b[0]))


def kernel(n_row, n_col, m_ref, v_ref, rot_ref, om_ref, ov_ref, mf, vf, rp, rr, rph, rpl, mrh, mrl,
           out_v, out_m, send_sem, recv_sem, loc_sem):
    height, width = m_ref.shape
    full = 2 * width
    shard = rot_ref.shape[1]
    n_y, n_z = n_row // 2, n_col // 4
    r, c = lax.axis_index("row"), lax.axis_index("col")
    y, h = lax.div(r, 2), lax.rem(r, 2)
    p, s = lax.div(c, 2), lax.rem(c, 2)
    z, l = lax.div(p, 2), lax.rem(p, 2)
    core, lane = (r, c + 1 - 2 * s), (r, c + 2 - 4 * l)
    z_next, z_last = (r, lax.rem(c + 4, n_col)), (r, lax.rem(c + n_col - 4, n_col))
    y_next, y_last = (lax.rem(r + 2, n_row), c), (lax.rem(r + n_row - 2, n_row), c)

    def source_z(at):
        return lax.rem(at - 2 * z + 2 * n_z, n_z)

    across = [(2 * lax.rem(2 * y + z, n_y) + (l if e == 0 else 1 - l), 2 * r + t) for e in range(2) for t in range(2)]
    across_from = [(p, 4 * source_z(y) + 2 * (h if e == 0 else 1 - h) + t) for e in range(2) for t in range(2)]
    across_self = [(to[0] == r) & (to[1] == c) for to in across]
    across_same = [(who[0] == r) & (who[1] == c) for who in across_from]
    col_to, col_from = target(c, n_col), origin(c, n_col)
    row_to = [target(2 * r + u, 2 * n_row) for u in range(2)]
    row_from = [origin(2 * r + u, 2 * n_row) for u in range(2)]
    v_to, v_from = (r, col_to), (r, col_from)
    v_self = col_to == c
    m_to = [(lax.div(row_to[u], 2), col_to) for u in range(2)]
    m_from = [(lax.div(row_from[u], 2), col_from) for u in range(2)]
    m_self = [(m_to[u][0] == r) & (col_to == c) for u in range(2)]
    m_same = [(m_from[u][0] == r) & (col_from == c) for u in range(2)]

    barrier = pltpu.get_barrier_semaphore()
    awaited = 6

    def greet(device):
        pl.semaphore_signal(barrier, inc=1, device_id=device, device_id_type=MESH)

    for device in (core, lane, z_next, z_last, y_next, y_last):
        greet(device)
    for same in (*across_self, v_self, *m_self):
        awaited = awaited + jnp.where(same, 0, 1)
    for device, same in (*zip(across_from, across_same), (v_from, v_self),
                         (m_from[0], m_same[0]), (m_from[1], m_same[1])):
        pl.when(jnp.logical_not(same))(functools.partial(greet, device))

    own = pltpu.make_async_copy(rot_ref.at[0], rr.at[z, l, s], loc_sem.at[0])
    own.start()
    own_m = pltpu.make_async_copy(m_ref, mf.at[:, pl.ds(pl.multiple_of(s * width, width), width)], loc_sem.at[1])
    own_v = pltpu.make_async_copy(v_ref, vf.at[:, pl.ds(pl.multiple_of(s * width, width), width)], loc_sem.at[2])
    own_m.start()
    own_v.start()
    pl.semaphore_wait(barrier, awaited)

    index = iter(range(200))
    sends = []

    def describe(src, dst, device, sem=None):
        sem = next(index) if sem is None else sem
        return pltpu.make_async_remote_copy(
            src_ref=src, dst_ref=dst, send_sem=send_sem.at[sem], recv_sem=recv_sem.at[sem],
            device_id=device, device_id_type=MESH)

    def send(src, dst, device):
        copy = describe(src, dst, device)
        copy.start()
        sends.append(copy)
        return copy

    crossed = []
    for i, device in enumerate(across):
        t = i % 2
        src = rot_ref.at[0, :, t * width:(t + 1) * width]
        sem = next(index)
        far = describe(src, rp.at[c], device, sem)
        near = pltpu.make_async_copy(src, rp.at[c], recv_sem.at[sem])
        pl.when(jnp.logical_not(across_self[i]))(far.start)
        pl.when(across_self[i])(near.start)
        crossed.append((far, across_self[i], sem))
    src = rot_ref.at[0]
    ring_z = {(0, d, 0): send(src, rr.at[z, l, s], device) for d, device in ((1, z_next), (-1, z_last))}
    to_lane = send(src, rr.at[z, l, s], lane)
    mine = pl.ds(pl.multiple_of(s * width, width), width)
    got_v = send(v_ref, vf.at[:, mine], core)
    got_m = send(m_ref, mf.at[:, mine], core)
    ring_y, core_z = {}, []

    def z_block(at, part):
        return rr.at[at, l if part == 0 else 1 - l, s]

    def y_block(at, part):
        return rp.at[4 * source_z(at) + 2 * (h if part < 2 else 1 - h) + part % 2]

    def ring(k, size, ring_of, place, pick, device_of, parts, every):
        far = size // 2
        for part in parts:
            for d in (1, -1):
                if k > 0:
                    if (k - 1, d, part) not in ring_of:
                        continue
                    ring_of[k - 1, d, part].wait_recv()
                block = pick(lax.rem(place - d * k + size, size), part)
                if k < far - 1 or (k == far - 1 and (d == 1) == (part < every // 2)):
                    ring_of[k, d, part] = send(block, block, device_of[d])

    def step_z(k, part):
        ring(k, n_z, ring_z, z, z_block, {1: z_next, -1: z_last}, (part,), 2)
        if part == 1 and k > 0:
            for d in (1, -1) if k < n_z // 2 else (1,):
                both = rr.at[lax.rem(z - d * k + n_z, n_z), :, s]
                core_z.append(send(both, both, core))

    def split_rp(at):
        high, low = halves(rp[pl.ds(4 * at, 4)].reshape(4 * shard, width))
        rows = pl.ds(pl.multiple_of(at * (4 * shard), 4 * shard), 4 * shard)
        rph[rows, :] = high
        rpl[rows, :] = low

    def step_y(k, side):
        ring(k, n_y, ring_y, y, y_block, {1: y_next, -1: y_last}, (2 * side, 2 * side + 1), 4)
        if side == 1:
            for d in (1, -1) if 0 < k < n_y // 2 else (1,):
                split_rp(source_z(lax.rem(y - d * k + n_y, n_y)))

    def arrived(e):
        block = rp.at[pl.ds(4 * source_z(y) + 2 * (h if e == 0 else 1 - h), 2)]
        for t in range(2):
            pl.when(s == t)(pltpu.make_async_copy(block, block, recv_sem.at[crossed[2 * e + t][2]]).wait)

    to_lane.wait_recv()
    step_z(0, 1)
    own.wait()
    both = rr.at[z, :, s]
    core_z.append(send(both, both, core))
    step_z(1, 0)
    arrived(0)
    step_y(0, 0)
    step_z(1, 1)
    step_z(2, 0)
    arrived(1)
    step_y(0, 1)
    for k in range(1, n_y // 2 + 1):
        step_y(k, 0)
        if k + 1 <= n_z // 2:
            step_z(k + 1, 1)
        if k + 2 <= n_z // 2:
            step_z(k + 2, 0)
        step_y(k, 1)
    own_v.wait()
    own_m.wait()
    got_v.wait_recv()
    got_m.wait_recv()

    step = 256 if height % 256 == 0 else height // 3
    v_sem = next(index)
    m_sem = [next(index) for _ in range(2)]

    def move(src, dst, device, same, sem):
        far = describe(src, dst, device, sem)
        pl.when(jnp.logical_not(same))(far.start)
        pl.when(same)(pltpu.make_async_copy(src, dst, recv_sem.at[sem]).start)

    @pl.loop(0, height // step)
    def _(i):
        at = pl.ds(pl.multiple_of(i * step, step), step)
        out_v[at, :] = product(halves(vf[at, :]), (rph[...], rpl[...]), (1,))
        move(out_v.at[at], ov_ref.at[at], v_to, v_self, v_sem)

    @pl.loop(0, height // step)
    def _(i):
        at = pl.ds(pl.multiple_of(i * step, step), step)
        high, low = halves(product(halves(mf[at, :]), (rph[...], rpl[...]), (1,)))
        mrh[at, :] = high
        mrl[at, :] = low

    for copy in core_z:
        copy.wait_recv()

    tile = 128 if width % 128 == 0 else width
    for u in range(2):
        slot = lax.rem(row_to[u], 2)
        dst_base = slot * width
        sem = jnp.where(slot == 0, m_sem[0], m_sem[1])

        @pl.loop(0, width // tile)
        def _(i):
            src_at = pl.multiple_of(u * width + i * tile, tile)
            part = rr[:, :, :, :, pl.ds(src_at, tile)].reshape(height, tile)
            at = pl.ds(src_at, tile)
            out_m[at, :] = product(halves(part), (mrh[...], mrl[...]), (0,))
            to = pl.ds(pl.multiple_of(dst_base + i * tile, tile), tile)
            move(out_m.at[at], om_ref.at[to], m_to[u], m_self[u], sem)

    pltpu.make_async_copy(ov_ref, ov_ref, recv_sem.at[v_sem]).wait()
    for u in range(2):
        part = om_ref.at[u * width:(u + 1) * width]
        pltpu.make_async_copy(part, part, recv_sem.at[m_sem[u]]).wait()
    for copy in sends:
        copy.wait_send()
    for far, same, _ in crossed:
        pl.when(jnp.logical_not(same))(far.wait_send)
    v_out = describe(out_v, ov_ref, v_to, v_sem)
    pl.when(jnp.logical_not(v_self))(v_out.wait_send)
    for u in range(2):
        slot = lax.rem(row_to[u], 2)
        sem = jnp.where(slot == 0, m_sem[0], m_sem[1])
        part = out_m.at[u * width:(u + 1) * width]
        out = describe(part, om_ref.at[0:width], m_to[u], sem)
        pl.when(jnp.logical_not(m_self[u]))(out.wait_send)


def solution(mesh):
    n_row, n_col = mesh.shape["row"], mesh.shape["col"]

    def on_device(matrix, vectors, rotations):
        height, width = matrix.shape
        shard = rotations.shape[1]
        any_space = pl.BlockSpec(memory_space=pl.ANY)
        return pl.pallas_call(
            functools.partial(kernel, n_row, n_col),
            out_shape=[jax.ShapeDtypeStruct((height, width), F32)] * 2,
            in_specs=[any_space] * 3,
            out_specs=[any_space] * 2,
            scratch_shapes=[
                pltpu.VMEM((height, 2 * width), F32),
                pltpu.VMEM((height, 2 * width), F32),
                pltpu.VMEM((n_col, shard, width), F32),
                pltpu.VMEM((n_col // 4, 2, 2, shard, 2 * width), F32),
                pltpu.VMEM((height, width), BF16),
                pltpu.VMEM((height, width), BF16),
                pltpu.VMEM((height, width), BF16),
                pltpu.VMEM((height, width), BF16),
                pltpu.VMEM((height, width), F32),
                pltpu.VMEM((height, width), F32),
                pltpu.SemaphoreType.DMA((80,)),
                pltpu.SemaphoreType.DMA((80,)),
                pltpu.SemaphoreType.DMA((3,)),
            ],
            compiler_params=pltpu.CompilerParams(
                collective_id=0, has_side_effects=True, vmem_limit_bytes=60 * 1024 * 1024),
            name="round",
        )(matrix, vectors, rotations)

    return jax.shard_map(
        on_device, mesh=mesh,
        in_specs=(P("row", "col"), P("row", "col"), P("row", "col", None)),
        out_specs=(P("row", "col"), P("row", "col")), check_vma=False)
```

```python
import functools

import jax
import jax.numpy as jnp
from jax import lax
from jax.experimental import pallas as pl
from jax.experimental.pallas import tpu as pltpu
from jax.sharding import PartitionSpec as P

MESH = pl.DeviceIdType.MESH
F32 = jnp.float32
BF16 = jnp.bfloat16


def target(k, count):
    moved = jnp.where(lax.rem(k, 2) == 0, k + 2, k - 2)
    moved = jnp.where(k == count - 2, count - 1, moved)
    moved = jnp.where(k == 1, 2, moved)
    return jnp.where(k == 0, 0, moved)


def origin(k, count):
    moved = jnp.where(lax.rem(k, 2) == 0, k - 2, k + 2)
    moved = jnp.where(k == count - 1, count - 2, moved)
    moved = jnp.where(k == 2, 1, moved)
    return jnp.where(k == 0, 0, moved)


def halves(value):
    high = value.astype(BF16)
    return high, (value - high.astype(F32)).astype(BF16)


def product(a, b, contract):
    dims = ((contract, (0,)), ((), ()))
    dot = functools.partial(lax.dot_general, dimension_numbers=dims, preferred_element_type=F32)
    return dot(a[0], b[0]) + (dot(a[0], b[1]) + dot(a[1], b[0]))


def kernel(n_row, n_col, m_ref, v_ref, rot_ref, om_ref, ov_ref, mf, vf, rp, rr, rph, rpl, mrh, mrl,
           out_v, out_m, passed, send_sem, recv_sem, loc_sem, pass_send, pass_recv):
    height, width = m_ref.shape
    full = 2 * width
    shard = rot_ref.shape[1]
    n_y, n_z = n_row // 2, n_col // 4
    r, c = lax.axis_index("row"), lax.axis_index("col")
    y, h = lax.div(r, 2), lax.rem(r, 2)
    p, s = lax.div(c, 2), lax.rem(c, 2)
    z, l = lax.div(p, 2), lax.rem(p, 2)
    core, lane = (r, c + 1 - 2 * s), (r, c + 2 - 4 * l)
    z_next, z_last = (r, lax.rem(c + 4, n_col)), (r, lax.rem(c + n_col - 4, n_col))
    y_next, y_last = (lax.rem(r + 2, n_row), c), (lax.rem(r + n_row - 2, n_row), c)

    def source_z(at):
        return lax.rem(at - 2 * z + 2 * n_z, n_z)

    across = [(2 * lax.rem(2 * y + z, n_y) + (l if e == 0 else 1 - l), 2 * r + t) for e in range(2) for t in range(2)]
    across_from = [(p, 4 * source_z(y) + 2 * (h if e == 0 else 1 - h) + t) for e in range(2) for t in range(2)]
    across_self = [(to[0] == r) & (to[1] == c) for to in across]
    across_same = [(who[0] == r) & (who[1] == c) for who in across_from]
    col_to, col_from = target(c, n_col), origin(c, n_col)
    row_to = [target(2 * r + u, 2 * n_row) for u in range(2)]
    row_from = [origin(2 * r + u, 2 * n_row) for u in range(2)]
    v_to, v_from = (r, col_to), (r, col_from)
    v_self = col_to == c
    m_to = [(lax.div(row_to[u], 2), col_to) for u in range(2)]
    m_from = [(lax.div(row_from[u], 2), col_from) for u in range(2)]
    m_self = [(m_to[u][0] == r) & (col_to == c) for u in range(2)]
    m_same = [(m_from[u][0] == r) & (col_from == c) for u in range(2)]

    def among(row):
        return (row == 1) | (row == n_row - 2)

    edge = (c == 0) | (c == n_col - 2)
    relayed = [among(m_to[u][0]) & edge & (lax.rem(row_to[u], 2) == 0) for u in range(2)]
    middle = [(m_to[u][0], jnp.where(c == 0, 2, n_col - 4)) for u in range(2)]
    relaying = among(r) & ((c == 2) | (c == n_col - 4))
    relay_from = (m_from[0][0], jnp.where(c == 2, 0, n_col - 2))
    relay_to = (r, jnp.where(c == 2, 0, n_col - 1))
    through = among(r) & ((c == 0) | (c == n_col - 1))
    m_giver = (jnp.where(through, r, m_from[0][0]),
               jnp.where(through, jnp.where(c == 0, 2, n_col - 4), col_from))

    barrier = pltpu.get_barrier_semaphore()
    awaited = 6

    def greet(device):
        pl.semaphore_signal(barrier, inc=1, device_id=device, device_id_type=MESH)

    for device in (core, lane, z_next, z_last, y_next, y_last):
        greet(device)
    for same in (*across_self, v_self, *m_self):
        awaited = awaited + jnp.where(same, 0, 1)
    for device, same in (*zip(across_from, across_same), (v_from, v_self),
                         (m_giver, m_same[0]), (m_from[1], m_same[1])):
        pl.when(jnp.logical_not(same))(functools.partial(greet, device))

    awaited = awaited + jnp.where(relaying, 1, 0)

    @pl.when(relaying)
    def _():
        greet(relay_from)

    own = pltpu.make_async_copy(rot_ref.at[0], rr.at[z, l, s], loc_sem.at[0])
    own.start()
    own_m = pltpu.make_async_copy(m_ref, mf.at[:, pl.ds(pl.multiple_of(s * width, width), width)], loc_sem.at[1])
    own_v = pltpu.make_async_copy(v_ref, vf.at[:, pl.ds(pl.multiple_of(s * width, width), width)], loc_sem.at[2])
    own_m.start()
    own_v.start()
    pl.semaphore_wait(barrier, awaited)

    index = iter(range(200))
    sends = []

    def describe(src, dst, device, sem=None):
        sem = next(index) if sem is None else sem
        return pltpu.make_async_remote_copy(
            src_ref=src, dst_ref=dst, send_sem=send_sem.at[sem], recv_sem=recv_sem.at[sem],
            device_id=device, device_id_type=MESH)

    def send(src, dst, device):
        copy = describe(src, dst, device)
        copy.start()
        sends.append(copy)
        return copy

    crossed = []
    for i, device in enumerate(across):
        t = i % 2
        src = rot_ref.at[0, :, t * width:(t + 1) * width]
        sem = next(index)
        far = describe(src, rp.at[c], device, sem)
        near = pltpu.make_async_copy(src, rp.at[c], recv_sem.at[sem])
        pl.when(jnp.logical_not(across_self[i]))(far.start)
        pl.when(across_self[i])(near.start)
        crossed.append((far, across_self[i], sem))
    src = rot_ref.at[0]
    ring_z = {(0, d, 0): send(src, rr.at[z, l, s], device) for d, device in ((1, z_next), (-1, z_last))}
    to_lane = send(src, rr.at[z, l, s], lane)
    mine = pl.ds(pl.multiple_of(s * width, width), width)
    got_v = send(v_ref, vf.at[:, mine], core)
    got_m = send(m_ref, mf.at[:, mine], core)
    ring_y, core_z = {}, []

    def z_block(at, part):
        return rr.at[at, l if part == 0 else 1 - l, s]

    def y_block(at, part):
        return rp.at[4 * source_z(at) + 2 * (h if part < 2 else 1 - h) + part % 2]

    def ring(k, size, ring_of, place, pick, device_of, parts, every):
        far = size // 2
        for part in parts:
            for d in (1, -1):
                if k > 0:
                    if (k - 1, d, part) not in ring_of:
                        continue
                    ring_of[k - 1, d, part].wait_recv()
                block = pick(lax.rem(place - d * k + size, size), part)
                if k < far - 1 or (k == far - 1 and (d == 1) == (part < every // 2)):
                    ring_of[k, d, part] = send(block, block, device_of[d])

    def step_z(k, part):
        ring(k, n_z, ring_z, z, z_block, {1: z_next, -1: z_last}, (part,), 2)
        if part == 1 and k > 0:
            for d in (1, -1) if k < n_z // 2 else (1,):
                both = rr.at[lax.rem(z - d * k + n_z, n_z), :, s]
                core_z.append(send(both, both, core))

    def split_rp(at):
        high, low = halves(rp[pl.ds(4 * at, 4)].reshape(4 * shard, width))
        rows = pl.ds(pl.multiple_of(at * (4 * shard), 4 * shard), 4 * shard)
        rph[rows, :] = high
        rpl[rows, :] = low

    def step_y(k, side):
        ring(k, n_y, ring_y, y, y_block, {1: y_next, -1: y_last}, (2 * side, 2 * side + 1), 4)
        if side == 1:
            for d in (1, -1) if 0 < k < n_y // 2 else (1,):
                split_rp(source_z(lax.rem(y - d * k + n_y, n_y)))

    def arrived(e):
        block = rp.at[pl.ds(4 * source_z(y) + 2 * (h if e == 0 else 1 - h), 2)]
        for t in range(2):
            pl.when(s == t)(pltpu.make_async_copy(block, block, recv_sem.at[crossed[2 * e + t][2]]).wait)

    to_lane.wait_recv()
    step_z(0, 1)
    own.wait()
    both = rr.at[z, :, s]
    core_z.append(send(both, both, core))
    step_z(1, 0)
    arrived(0)
    step_y(0, 0)
    step_z(1, 1)
    step_z(2, 0)
    arrived(1)
    step_y(0, 1)
    for k in range(1, n_y // 2 + 1):
        step_y(k, 0)
        if k + 1 <= n_z // 2:
            step_z(k + 1, 1)
        if k + 2 <= n_z // 2:
            step_z(k + 2, 0)
        step_y(k, 1)
    own_v.wait()
    own_m.wait()
    got_v.wait_recv()
    got_m.wait_recv()

    step = 256 if height % 256 == 0 else height // 3
    v_sem = next(index)
    m_sem = [next(index) for _ in range(2)]

    def move(src, dst, device, same, sem):
        far = describe(src, dst, device, sem)
        pl.when(jnp.logical_not(same))(far.start)
        pl.when(same)(pltpu.make_async_copy(src, dst, recv_sem.at[sem]).start)

    def turn():
        @pl.loop(0, height // step)
        def _(i):
            at = pl.ds(pl.multiple_of(i * step, step), step)
            out_v[at, :] = product(halves(vf[at, :]), (rph[...], rpl[...]), (1,))
            move(out_v.at[at], ov_ref.at[at], v_to, v_self, v_sem)

    pl.when(jnp.logical_not(edge))(turn)

    @pl.loop(0, height // step)
    def _(i):
        at = pl.ds(pl.multiple_of(i * step, step), step)
        high, low = halves(product(halves(mf[at, :]), (rph[...], rpl[...]), (1,)))
        mrh[at, :] = high
        mrl[at, :] = low

    for copy in core_z:
        copy.wait_recv()

    tile = 128 if width % 128 == 0 else width
    pieces = width // tile
    for u in range(2):
        slot = lax.rem(row_to[u], 2)
        dst_base = slot * width
        sem = jnp.where(slot == 0, m_sem[0], m_sem[1])

        @pl.loop(0, width // tile)
        def _(i):
            src_at = pl.multiple_of(u * width + i * tile, tile)
            part = rr[:, :, :, :, pl.ds(src_at, tile)].reshape(height, tile)
            at = pl.ds(src_at, tile)
            out_m[at, :] = product(halves(part), (mrh[...], mrl[...]), (0,))
            to = pl.ds(pl.multiple_of(dst_base + i * tile, tile), tile)
            pl.when(jnp.logical_not(relayed[u]))(
                functools.partial(move, out_m.at[at], om_ref.at[to], m_to[u], m_self[u], sem))

            @pl.when(relayed[u])
            def _():
                pltpu.make_async_remote_copy(
                    src_ref=out_m.at[at], dst_ref=passed.at[pl.ds(pl.multiple_of(i * tile, tile), tile)], send_sem=send_sem.at[sem],
                    recv_sem=pass_recv.at[i], device_id=middle[u], device_id_type=MESH).start()

    pl.when(edge)(turn)

    def passing(i):
        at = pl.ds(i * tile, tile)
        return pltpu.make_async_remote_copy(
            src_ref=passed.at[at], dst_ref=om_ref.at[at], send_sem=pass_send.at[i], recv_sem=recv_sem.at[m_sem[0]],
            device_id=relay_to, device_id_type=MESH)

    @pl.when(relaying)
    def _():
        for i in range(pieces):
            at = pl.ds(i * tile, tile)
            pltpu.make_async_copy(passed.at[at], passed.at[at], pass_recv.at[i]).wait()
            passing(i).start()
        for i in range(pieces):
            passing(i).wait_send()

    pltpu.make_async_copy(ov_ref, ov_ref, recv_sem.at[v_sem]).wait()
    for u in range(2):
        part = om_ref.at[u * width:(u + 1) * width]
        pltpu.make_async_copy(part, part, recv_sem.at[m_sem[u]]).wait()
    for copy in sends:
        copy.wait_send()
    for far, same, _ in crossed:
        pl.when(jnp.logical_not(same))(far.wait_send)
    v_out = describe(out_v, ov_ref, v_to, v_sem)
    pl.when(jnp.logical_not(v_self))(v_out.wait_send)
    for u in range(2):
        slot = lax.rem(row_to[u], 2)
        sem = jnp.where(slot == 0, m_sem[0], m_sem[1])
        part = out_m.at[u * width:(u + 1) * width]
        out = describe(part, om_ref.at[0:width], m_to[u], sem)
        pl.when(jnp.logical_not(m_self[u]))(out.wait_send)


def solution(mesh):
    n_row, n_col = mesh.shape["row"], mesh.shape["col"]

    def on_device(matrix, vectors, rotations):
        height, width = matrix.shape
        shard = rotations.shape[1]
        any_space = pl.BlockSpec(memory_space=pl.ANY)
        return pl.pallas_call(
            functools.partial(kernel, n_row, n_col),
            out_shape=[jax.ShapeDtypeStruct((height, width), F32)] * 2,
            in_specs=[any_space] * 3,
            out_specs=[any_space] * 2,
            scratch_shapes=[
                pltpu.VMEM((height, 2 * width), F32),
                pltpu.VMEM((height, 2 * width), F32),
                pltpu.VMEM((n_col, shard, width), F32),
                pltpu.VMEM((n_col // 4, 2, 2, shard, 2 * width), F32),
                pltpu.VMEM((height, width), BF16),
                pltpu.VMEM((height, width), BF16),
                pltpu.VMEM((height, width), BF16),
                pltpu.VMEM((height, width), BF16),
                pltpu.VMEM((height, width), F32),
                pltpu.VMEM((height, width), F32),
                pltpu.VMEM((width, width), F32),
                pltpu.SemaphoreType.DMA((80,)),
                pltpu.SemaphoreType.DMA((80,)),
                pltpu.SemaphoreType.DMA((3,)),
                pltpu.SemaphoreType.DMA((width // 128,)),
                pltpu.SemaphoreType.DMA((width // 128,)),
            ],
            compiler_params=pltpu.CompilerParams(
                collective_id=0, has_side_effects=True, vmem_limit_bytes=60 * 1024 * 1024),
            name="round",
        )(matrix, vectors, rotations)

    return jax.shard_map(
        on_device, mesh=mesh,
        in_specs=(P("row", "col"), P("row", "col"), P("row", "col", None)),
        out_specs=(P("row", "col"), P("row", "col")), check_vma=False)
```

```python
import functools

import jax
import jax.numpy as jnp
from jax import lax
from jax.experimental import pallas as pl
from jax.experimental.pallas import tpu as pltpu
from jax.sharding import PartitionSpec as P

MESH = pl.DeviceIdType.MESH
F32 = jnp.float32
BF16 = jnp.bfloat16


def target(k, count):
    moved = jnp.where(lax.rem(k, 2) == 0, k + 2, k - 2)
    moved = jnp.where(k == count - 2, count - 1, moved)
    moved = jnp.where(k == 1, 2, moved)
    return jnp.where(k == 0, 0, moved)


def origin(k, count):
    moved = jnp.where(lax.rem(k, 2) == 0, k - 2, k + 2)
    moved = jnp.where(k == count - 1, count - 2, moved)
    moved = jnp.where(k == 2, 1, moved)
    return jnp.where(k == 0, 0, moved)


def halves(value):
    high = value.astype(BF16)
    return high, (value - high.astype(F32)).astype(BF16)


def product(a, b, contract):
    dims = ((contract, (0,)), ((), ()))
    dot = functools.partial(lax.dot_general, dimension_numbers=dims, preferred_element_type=F32)
    return dot(a[0], b[0]) + (dot(a[0], b[1]) + dot(a[1], b[0]))


def kernel(n_row, n_col, m_ref, v_ref, rot_ref, om_ref, ov_ref, mf, vf, rp, rr, rph, rpl, mrh, mrl,
           out_v, out_m, passed, send_sem, recv_sem, loc_sem, pass_send, pass_recv):
    height, width = m_ref.shape
    full = 2 * width
    shard = rot_ref.shape[1]
    n_y, n_z = n_row // 2, n_col // 4
    r, c = lax.axis_index("row"), lax.axis_index("col")
    y, h = lax.div(r, 2), lax.rem(r, 2)
    p, s = lax.div(c, 2), lax.rem(c, 2)
    z, l = lax.div(p, 2), lax.rem(p, 2)
    core, lane = (r, c + 1 - 2 * s), (r, c + 2 - 4 * l)
    z_next, z_last = (r, lax.rem(c + 4, n_col)), (r, lax.rem(c + n_col - 4, n_col))
    y_next, y_last = (lax.rem(r + 2, n_row), c), (lax.rem(r + n_row - 2, n_row), c)

    def source_z(at):
        return lax.rem(at - 2 * z + 2 * n_z, n_z)

    y_far = {d: (lax.rem(r + n_row + 4 * d, n_row), c) for d in (1, -1)}
    z_far = {d: (r, lax.rem(c + n_col + 8 * d, n_col)) for d in (1, -1)}
    across = [(2 * lax.rem(2 * y + z, n_y) + (l if e == 0 else 1 - l), 2 * r + t) for e in range(2) for t in range(2)]
    across_from = [(p, 4 * source_z(y) + 2 * (h if e == 0 else 1 - h) + t) for e in range(2) for t in range(2)]
    across_self = [(to[0] == r) & (to[1] == c) for to in across]
    across_same = [(who[0] == r) & (who[1] == c) for who in across_from]
    col_to, col_from = target(c, n_col), origin(c, n_col)
    row_to = [target(2 * r + u, 2 * n_row) for u in range(2)]
    row_from = [origin(2 * r + u, 2 * n_row) for u in range(2)]
    v_to, v_from = (r, col_to), (r, col_from)
    v_self = col_to == c
    m_to = [(lax.div(row_to[u], 2), col_to) for u in range(2)]
    m_from = [(lax.div(row_from[u], 2), col_from) for u in range(2)]
    m_self = [(m_to[u][0] == r) & (col_to == c) for u in range(2)]
    m_same = [(m_from[u][0] == r) & (col_from == c) for u in range(2)]

    def among(row):
        return (row == 1) | (row == n_row - 2)

    edge = (c == 0) | (c == n_col - 2)
    relayed = [among(m_to[u][0]) & edge & (lax.rem(row_to[u], 2) == 0) for u in range(2)]
    middle = [(m_to[u][0], jnp.where(c == 0, 2, n_col - 4)) for u in range(2)]
    relaying = among(r) & ((c == 2) | (c == n_col - 4))
    relay_from = (m_from[0][0], jnp.where(c == 2, 0, n_col - 2))
    relay_to = (r, jnp.where(c == 2, 0, n_col - 1))
    through = among(r) & ((c == 0) | (c == n_col - 1))
    m_giver = (jnp.where(through, r, m_from[0][0]),
               jnp.where(through, jnp.where(c == 0, 2, n_col - 4), col_from))

    barrier = pltpu.get_barrier_semaphore()
    awaited = 10

    def greet(device):
        pl.semaphore_signal(barrier, inc=1, device_id=device, device_id_type=MESH)

    for device in (core, lane, z_next, z_last, y_next, y_last, *y_far.values(), *z_far.values()):
        greet(device)
    for same in (*across_self, v_self, *m_self):
        awaited = awaited + jnp.where(same, 0, 1)
    for device, same in (*zip(across_from, across_same), (v_from, v_self),
                         (m_giver, m_same[0]), (m_from[1], m_same[1])):
        pl.when(jnp.logical_not(same))(functools.partial(greet, device))

    awaited = awaited + jnp.where(relaying, 1, 0)

    @pl.when(relaying)
    def _():
        greet(relay_from)

    own = pltpu.make_async_copy(rot_ref.at[0], rr.at[z, l, s], loc_sem.at[0])
    own.start()
    own_m = pltpu.make_async_copy(m_ref, mf.at[:, pl.ds(pl.multiple_of(s * width, width), width)], loc_sem.at[1])
    own_v = pltpu.make_async_copy(v_ref, vf.at[:, pl.ds(pl.multiple_of(s * width, width), width)], loc_sem.at[2])
    own_m.start()
    own_v.start()
    pl.semaphore_wait(barrier, awaited)

    index = iter(range(200))
    sends = []

    def describe(src, dst, device, sem=None):
        sem = next(index) if sem is None else sem
        return pltpu.make_async_remote_copy(
            src_ref=src, dst_ref=dst, send_sem=send_sem.at[sem], recv_sem=recv_sem.at[sem],
            device_id=device, device_id_type=MESH)

    def send(src, dst, device):
        copy = describe(src, dst, device)
        copy.start()
        sends.append(copy)
        return copy

    crossed = []
    for i, device in enumerate(across):
        t = i % 2
        src = rot_ref.at[0, :, t * width:(t + 1) * width]
        sem = next(index)
        far = describe(src, rp.at[c], device, sem)
        near = pltpu.make_async_copy(src, rp.at[c], recv_sem.at[sem])
        pl.when(jnp.logical_not(across_self[i]))(far.start)
        pl.when(across_self[i])(near.start)
        crossed.append((far, across_self[i], sem))
    src = rot_ref.at[0]
    ring_z = {(0, d, 0): send(src, rr.at[z, l, s], device) for d, device in ((1, z_next), (-1, z_last))}
    to_lane = send(src, rr.at[z, l, s], lane)
    mine = pl.ds(pl.multiple_of(s * width, width), width)
    got_v = send(v_ref, vf.at[:, mine], core)
    got_m = send(m_ref, mf.at[:, mine], core)
    ring_y, core_z = {}, []

    def z_block(at, part):
        return rr.at[at, l if part == 0 else 1 - l, s]

    def y_block(at, part):
        return rp.at[4 * source_z(at) + 2 * (h if part < 2 else 1 - h) + part % 2]

    def ring(k, size, ring_of, place, pick, device_of, far_of, parts, every):
        far = size // 2
        for part in parts:
            for d in (1, -1):
                if k > 0:
                    if (k - 1, d, part) not in ring_of:
                        continue
                    ring_of[k - 1, d, part].wait_recv()
                block = pick(lax.rem(place - d * k + size, size), part)
                if k < far - 1:
                    ring_of[k, d, part] = send(block, block, device_of[d])
                if k == far - 2 and (d == 1) == (part < every // 2):
                    ring_of[k + 1, d, part] = send(block, block, far_of[d])

    def step_z(k, part):
        ring(k, n_z, ring_z, z, z_block, {1: z_next, -1: z_last}, z_far, (part,), 2)
        if part == 1 and k > 0:
            for d in (1, -1) if k < n_z // 2 else (1,):
                both = rr.at[lax.rem(z - d * k + n_z, n_z), :, s]
                core_z.append(send(both, both, core))

    def split_rp(at):
        high, low = halves(rp[pl.ds(4 * at, 4)].reshape(4 * shard, width))
        rows = pl.ds(pl.multiple_of(at * (4 * shard), 4 * shard), 4 * shard)
        rph[rows, :] = high
        rpl[rows, :] = low

    def step_y(k, side):
        ring(k, n_y, ring_y, y, y_block, {1: y_next, -1: y_last}, y_far, (2 * side, 2 * side + 1), 4)
        if side == 1:
            for d in (1, -1) if 0 < k < n_y // 2 else (1,):
                split_rp(source_z(lax.rem(y - d * k + n_y, n_y)))

    def arrived(e):
        block = rp.at[pl.ds(4 * source_z(y) + 2 * (h if e == 0 else 1 - h), 2)]
        for t in range(2):
            pl.when(s == t)(pltpu.make_async_copy(block, block, recv_sem.at[crossed[2 * e + t][2]]).wait)

    to_lane.wait_recv()
    step_z(0, 1)
    own.wait()
    both = rr.at[z, :, s]
    core_z.append(send(both, both, core))
    step_z(1, 0)
    arrived(0)
    step_y(0, 0)
    step_z(1, 1)
    step_z(2, 0)
    arrived(1)
    step_y(0, 1)
    for k in range(1, n_y // 2 + 1):
        step_y(k, 0)
        if k + 1 <= n_z // 2:
            step_z(k + 1, 1)
        if k + 2 <= n_z // 2:
            step_z(k + 2, 0)
        step_y(k, 1)
    own_v.wait()
    own_m.wait()
    got_v.wait_recv()
    got_m.wait_recv()

    step = 256 if height % 256 == 0 else height // 3
    v_sem = next(index)
    m_sem = [next(index) for _ in range(2)]

    def move(src, dst, device, same, sem):
        far = describe(src, dst, device, sem)
        pl.when(jnp.logical_not(same))(far.start)
        pl.when(same)(pltpu.make_async_copy(src, dst, recv_sem.at[sem]).start)

    def turn():
        @pl.loop(0, height // step)
        def _(i):
            at = pl.ds(pl.multiple_of(i * step, step), step)
            out_v[at, :] = product(halves(vf[at, :]), (rph[...], rpl[...]), (1,))
            move(out_v.at[at], ov_ref.at[at], v_to, v_self, v_sem)

    pl.when(jnp.logical_not(edge))(turn)

    @pl.loop(0, height // step)
    def _(i):
        at = pl.ds(pl.multiple_of(i * step, step), step)
        high, low = halves(product(halves(mf[at, :]), (rph[...], rpl[...]), (1,)))
        mrh[at, :] = high
        mrl[at, :] = low

    for copy in core_z:
        copy.wait_recv()

    tile = 128 if width % 128 == 0 else width
    pieces = width // tile
    for u in range(2):
        slot = lax.rem(row_to[u], 2)
        dst_base = slot * width
        sem = jnp.where(slot == 0, m_sem[0], m_sem[1])

        @pl.loop(0, width // tile)
        def _(i):
            src_at = pl.multiple_of(u * width + i * tile, tile)
            part = rr[:, :, :, :, pl.ds(src_at, tile)].reshape(height, tile)
            at = pl.ds(src_at, tile)
            out_m[at, :] = product(halves(part), (mrh[...], mrl[...]), (0,))
            to = pl.ds(pl.multiple_of(dst_base + i * tile, tile), tile)
            pl.when(jnp.logical_not(relayed[u]))(
                functools.partial(move, out_m.at[at], om_ref.at[to], m_to[u], m_self[u], sem))

            @pl.when(relayed[u])
            def _():
                pltpu.make_async_remote_copy(
                    src_ref=out_m.at[at], dst_ref=passed.at[pl.ds(pl.multiple_of(i * tile, tile), tile)], send_sem=send_sem.at[sem],
                    recv_sem=pass_recv.at[i], device_id=middle[u], device_id_type=MESH).start()

    pl.when(edge)(turn)

    def passing(i):
        at = pl.ds(i * tile, tile)
        return pltpu.make_async_remote_copy(
            src_ref=passed.at[at], dst_ref=om_ref.at[at], send_sem=pass_send.at[i], recv_sem=recv_sem.at[m_sem[0]],
            device_id=relay_to, device_id_type=MESH)

    @pl.when(relaying)
    def _():
        for i in range(pieces):
            at = pl.ds(i * tile, tile)
            pltpu.make_async_copy(passed.at[at], passed.at[at], pass_recv.at[i]).wait()
            passing(i).start()
        for i in range(pieces):
            passing(i).wait_send()

    pltpu.make_async_copy(ov_ref, ov_ref, recv_sem.at[v_sem]).wait()
    for u in range(2):
        part = om_ref.at[u * width:(u + 1) * width]
        pltpu.make_async_copy(part, part, recv_sem.at[m_sem[u]]).wait()
    for copy in sends:
        copy.wait_send()
    for far, same, _ in crossed:
        pl.when(jnp.logical_not(same))(far.wait_send)
    v_out = describe(out_v, ov_ref, v_to, v_sem)
    pl.when(jnp.logical_not(v_self))(v_out.wait_send)
    for u in range(2):
        slot = lax.rem(row_to[u], 2)
        sem = jnp.where(slot == 0, m_sem[0], m_sem[1])
        part = out_m.at[u * width:(u + 1) * width]
        out = describe(part, om_ref.at[0:width], m_to[u], sem)
        pl.when(jnp.logical_not(m_self[u]))(out.wait_send)


def settle(*refs):
    given, out, (held, came, left) = refs[:2], refs[2:4], refs[4:]
    parts = came.shape[1]
    rows = given[0].shape[0] // parts
    pieces = [(a, i, slice(i * rows, (i + 1) * rows)) for i in range(parts) for a in range(2)]
    fetch = [pltpu.make_async_copy(given[a].at[at], held.at[a, at], came.at[a, i]) for a, i, at in pieces]
    store = [pltpu.make_async_copy(held.at[a, at], out[a].at[at], left.at[a, i]) for a, i, at in pieces]
    for copy in fetch:
        copy.start()
    for first, second in zip(fetch, store):
        first.wait()
        second.start()
    for copy in store:
        copy.wait()


def solution(mesh):
    n_row, n_col = mesh.shape["row"], mesh.shape["col"]

    def on_device(matrix, vectors, rotations):
        height, width = matrix.shape
        shard = rotations.shape[1]
        any_space = pl.BlockSpec(memory_space=pl.ANY)
        moved = pl.pallas_call(
            functools.partial(kernel, n_row, n_col),
            out_shape=[jax.ShapeDtypeStruct((height, width), F32)] * 2,
            in_specs=[any_space] * 3,
            out_specs=[any_space] * 2,
            scratch_shapes=[
                pltpu.VMEM((height, 2 * width), F32),
                pltpu.VMEM((height, 2 * width), F32),
                pltpu.VMEM((n_col, shard, width), F32),
                pltpu.VMEM((n_col // 4, 2, 2, shard, 2 * width), F32),
                pltpu.VMEM((height, width), BF16),
                pltpu.VMEM((height, width), BF16),
                pltpu.VMEM((height, width), BF16),
                pltpu.VMEM((height, width), BF16),
                pltpu.VMEM((height, width), F32),
                pltpu.VMEM((height, width), F32),
                pltpu.VMEM((width, width), F32),
                pltpu.SemaphoreType.DMA((80,)),
                pltpu.SemaphoreType.DMA((80,)),
                pltpu.SemaphoreType.DMA((3,)),
                pltpu.SemaphoreType.DMA((width // 128,)),
                pltpu.SemaphoreType.DMA((width // 128,)),
            ],
            compiler_params=pltpu.CompilerParams(
                collective_id=0, has_side_effects=True, vmem_limit_bytes=60 * 1024 * 1024),
            name="round",
        )(matrix, vectors, rotations)
        return pl.pallas_call(
            settle,
            out_shape=[jax.ShapeDtypeStruct((height, width), F32)] * 2,
            in_specs=[any_space] * 2,
            out_specs=[any_space] * 2,
            scratch_shapes=[
                pltpu.VMEM((2, height, width), F32),
                pltpu.SemaphoreType.DMA((2, 4)),
                pltpu.SemaphoreType.DMA((2, 4)),
            ],
            compiler_params=pltpu.CompilerParams(vmem_limit_bytes=60 * 1024 * 1024),
            name="settle",
        )(*moved)

    return jax.shard_map(
        on_device, mesh=mesh,
        in_specs=(P("row", "col"), P("row", "col"), P("row", "col", None)),
        out_specs=(P("row", "col"), P("row", "col")), check_vma=False)
```

```python
import functools

import jax
import jax.numpy as jnp
from jax import lax
from jax.experimental import pallas as pl
from jax.experimental.pallas import tpu as pltpu
from jax.sharding import PartitionSpec as P

MESH = pl.DeviceIdType.MESH
F32 = jnp.float32
BF16 = jnp.bfloat16


def target(k, count):
    moved = jnp.where(lax.rem(k, 2) == 0, k + 2, k - 2)
    moved = jnp.where(k == count - 2, count - 1, moved)
    moved = jnp.where(k == 1, 2, moved)
    return jnp.where(k == 0, 0, moved)


def origin(k, count):
    moved = jnp.where(lax.rem(k, 2) == 0, k - 2, k + 2)
    moved = jnp.where(k == count - 1, count - 2, moved)
    moved = jnp.where(k == 2, 1, moved)
    return jnp.where(k == 0, 0, moved)


def halves(value):
    high = value.astype(BF16)
    return high, (value - high.astype(F32)).astype(BF16)


def product(a, b, contract):
    dims = ((contract, (0,)), ((), ()))
    dot = functools.partial(lax.dot_general, dimension_numbers=dims, preferred_element_type=F32)
    return dot(a[0], b[0]) + (dot(a[0], b[1]) + dot(a[1], b[0]))


def kernel(n_row, n_col, m_ref, v_ref, rot_ref, om_ref, ov_ref, mf, vf, rp, rr, rph, rpl, mrh, mrl,
           out_v, out_m, passed, send_sem, recv_sem, loc_sem, pass_send, pass_recv):
    height, width = m_ref.shape
    full = 2 * width
    shard = rot_ref.shape[1]
    n_y, n_z = n_row // 2, n_col // 4
    r, c = lax.axis_index("row"), lax.axis_index("col")
    y, h = lax.div(r, 2), lax.rem(r, 2)
    p, s = lax.div(c, 2), lax.rem(c, 2)
    z, l = lax.div(p, 2), lax.rem(p, 2)
    core, lane = (r, c + 1 - 2 * s), (r, c + 2 - 4 * l)
    z_next, z_last = (r, lax.rem(c + 4, n_col)), (r, lax.rem(c + n_col - 4, n_col))
    y_next, y_last = (lax.rem(r + 2, n_row), c), (lax.rem(r + n_row - 2, n_row), c)

    def source_z(at):
        return lax.rem(at - 2 * z + 2 * n_z, n_z)

    y_far = {d: (lax.rem(r + n_row + 4 * d, n_row), c) for d in (1, -1)}
    z_far = {d: (r, lax.rem(c + n_col + 8 * d, n_col)) for d in (1, -1)}
    across = [(2 * lax.rem(2 * y + z, n_y) + (l if e == 0 else 1 - l), 2 * r + t) for e in range(2) for t in range(2)]
    across_from = [(p, 4 * source_z(y) + 2 * (h if e == 0 else 1 - h) + t) for e in range(2) for t in range(2)]
    across_self = [(to[0] == r) & (to[1] == c) for to in across]
    across_same = [(who[0] == r) & (who[1] == c) for who in across_from]
    col_to, col_from = target(c, n_col), origin(c, n_col)
    row_to = [target(2 * r + u, 2 * n_row) for u in range(2)]
    row_from = [origin(2 * r + u, 2 * n_row) for u in range(2)]
    v_to, v_from = (r, col_to), (r, col_from)
    v_self = col_to == c
    m_to = [(lax.div(row_to[u], 2), col_to) for u in range(2)]
    m_from = [(lax.div(row_from[u], 2), col_from) for u in range(2)]
    m_self = [(m_to[u][0] == r) & (col_to == c) for u in range(2)]
    m_same = [(m_from[u][0] == r) & (col_from == c) for u in range(2)]

    def among(row):
        return (row == 1) | (row == n_row - 2)

    edge = (c == 0) | (c == n_col - 2)
    relayed = [among(m_to[u][0]) & edge & (lax.rem(row_to[u], 2) == 0) for u in range(2)]
    middle = [(m_to[u][0], jnp.where(c == 0, 2, n_col - 4)) for u in range(2)]
    relaying = among(r) & ((c == 2) | (c == n_col - 4))
    relay_from = (m_from[0][0], jnp.where(c == 2, 0, n_col - 2))
    relay_to = (r, jnp.where(c == 2, 0, n_col - 1))
    through = among(r) & ((c == 0) | (c == n_col - 1))
    m_giver = (jnp.where(through, r, m_from[0][0]),
               jnp.where(through, jnp.where(c == 0, 2, n_col - 4), col_from))

    barrier = pltpu.get_barrier_semaphore()
    awaited = 10

    def greet(device):
        pl.semaphore_signal(barrier, inc=1, device_id=device, device_id_type=MESH)

    for device in (core, lane, z_next, z_last, y_next, y_last, *y_far.values(), *z_far.values()):
        greet(device)
    for same in (*across_self, v_self, *m_self):
        awaited = awaited + jnp.where(same, 0, 1)
    for device, same in (*zip(across_from, across_same), (v_from, v_self),
                         (m_giver, m_same[0]), (m_from[1], m_same[1])):
        pl.when(jnp.logical_not(same))(functools.partial(greet, device))

    awaited = awaited + jnp.where(relaying, 1, 0)

    @pl.when(relaying)
    def _():
        greet(relay_from)

    own = pltpu.make_async_copy(rot_ref.at[0], rr.at[z, l, s], loc_sem.at[0])
    own.start()
    own_m = pltpu.make_async_copy(m_ref, mf.at[:, pl.ds(pl.multiple_of(s * width, width), width)], loc_sem.at[1])
    own_v = pltpu.make_async_copy(v_ref, vf.at[:, pl.ds(pl.multiple_of(s * width, width), width)], loc_sem.at[2])
    own_m.start()
    own_v.start()
    pl.semaphore_wait(barrier, awaited)

    index = iter(range(200))
    sends = []

    def describe(src, dst, device, sem=None):
        sem = next(index) if sem is None else sem
        return pltpu.make_async_remote_copy(
            src_ref=src, dst_ref=dst, send_sem=send_sem.at[sem], recv_sem=recv_sem.at[sem],
            device_id=device, device_id_type=MESH)

    def send(src, dst, device):
        copy = describe(src, dst, device)
        copy.start()
        sends.append(copy)
        return copy

    crossed = []
    for i, device in enumerate(across):
        t = i % 2
        src = rot_ref.at[0, :, t * width:(t + 1) * width]
        sem = next(index)
        far = describe(src, rp.at[c], device, sem)
        near = pltpu.make_async_copy(src, rp.at[c], recv_sem.at[sem])
        pl.when(jnp.logical_not(across_self[i]))(far.start)
        pl.when(across_self[i])(near.start)
        crossed.append((far, across_self[i], sem))
    src = rot_ref.at[0]
    ring_z = {(0, d, 0): send(src, rr.at[z, l, s], device) for d, device in ((1, z_next), (-1, z_last))}
    to_lane = send(src, rr.at[z, l, s], lane)
    mine = pl.ds(pl.multiple_of(s * width, width), width)
    got_v = send(v_ref, vf.at[:, mine], core)
    got_m = send(m_ref, mf.at[:, mine], core)
    ring_y, core_z = {}, []

    def z_block(at, part):
        return rr.at[at, l if part == 0 else 1 - l, s]

    def y_block(at, part):
        return rp.at[4 * source_z(at) + 2 * (h if part < 2 else 1 - h) + part % 2]

    def ring(k, size, ring_of, place, pick, device_of, far_of, parts, every):
        far = size // 2
        for part in parts:
            for d in (1, -1):
                if k > 0:
                    if (k - 1, d, part) not in ring_of:
                        continue
                    ring_of[k - 1, d, part].wait_recv()
                block = pick(lax.rem(place - d * k + size, size), part)
                if k < far - 1:
                    ring_of[k, d, part] = send(block, block, device_of[d])
                if k == far - 2 and (d == 1) == (part < every // 2):
                    ring_of[k + 1, d, part] = send(block, block, far_of[d])

    def step_z(k, part):
        ring(k, n_z, ring_z, z, z_block, {1: z_next, -1: z_last}, z_far, (part,), 2)
        if part == 1 and k > 0:
            for d in (1, -1) if k < n_z // 2 else (1,):
                both = rr.at[lax.rem(z - d * k + n_z, n_z), :, s]
                core_z.append(send(both, both, core))

    def split_rp(at):
        high, low = halves(rp[pl.ds(4 * at, 4)].reshape(4 * shard, width))
        rows = pl.ds(pl.multiple_of(at * (4 * shard), 4 * shard), 4 * shard)
        rph[rows, :] = high
        rpl[rows, :] = low

    def step_y(k, side):
        ring(k, n_y, ring_y, y, y_block, {1: y_next, -1: y_last}, y_far, (2 * side, 2 * side + 1), 4)
        if side == 1:
            for d in (1, -1) if 0 < k < n_y // 2 else (1,):
                split_rp(source_z(lax.rem(y - d * k + n_y, n_y)))

    def arrived(e):
        block = rp.at[pl.ds(4 * source_z(y) + 2 * (h if e == 0 else 1 - h), 2)]
        for t in range(2):
            pl.when(s == t)(pltpu.make_async_copy(block, block, recv_sem.at[crossed[2 * e + t][2]]).wait)

    to_lane.wait_recv()
    step_z(0, 1)
    own.wait()
    both = rr.at[z, :, s]
    core_z.append(send(both, both, core))
    step_z(1, 0)
    arrived(0)
    step_y(0, 0)
    step_z(1, 1)
    step_z(2, 0)
    arrived(1)
    step_y(0, 1)
    for k in range(1, n_y // 2 + 1):
        step_y(k, 0)
        if k + 1 <= n_z // 2:
            step_z(k + 1, 1)
        if k + 2 <= n_z // 2:
            step_z(k + 2, 0)
        step_y(k, 1)
    own_v.wait()
    own_m.wait()
    got_v.wait_recv()
    got_m.wait_recv()

    step = 128 if height % 128 == 0 else height // 3
    v_sem = next(index)
    m_sem = [next(index) for _ in range(2)]

    def move(src, dst, device, same, sem):
        far = describe(src, dst, device, sem)
        pl.when(jnp.logical_not(same))(far.start)
        pl.when(same)(pltpu.make_async_copy(src, dst, recv_sem.at[sem]).start)

    def turn():
        @pl.loop(0, height // step)
        def _(i):
            at = pl.ds(pl.multiple_of(i * step, step), step)
            out_v[at, :] = product(halves(vf[at, :]), (rph[...], rpl[...]), (1,))
            move(out_v.at[at], ov_ref.at[at], v_to, v_self, v_sem)

    pl.when(jnp.logical_not(edge))(turn)

    @pl.loop(0, height // step)
    def _(i):
        at = pl.ds(pl.multiple_of(i * step, step), step)
        high, low = halves(product(halves(mf[at, :]), (rph[...], rpl[...]), (1,)))
        mrh[at, :] = high
        mrl[at, :] = low

    for copy in core_z:
        copy.wait_recv()

    tile = 128 if width % 128 == 0 else width
    pieces = width // tile
    for u in range(2):
        slot = lax.rem(row_to[u], 2)
        dst_base = slot * width
        sem = jnp.where(slot == 0, m_sem[0], m_sem[1])

        @pl.loop(0, width // tile)
        def _(i):
            src_at = pl.multiple_of(u * width + i * tile, tile)
            part = rr[:, :, :, :, pl.ds(src_at, tile)].reshape(height, tile)
            at = pl.ds(src_at, tile)
            out_m[at, :] = product(halves(part), (mrh[...], mrl[...]), (0,))
            to = pl.ds(pl.multiple_of(dst_base + i * tile, tile), tile)
            pl.when(jnp.logical_not(relayed[u]))(
                functools.partial(move, out_m.at[at], om_ref.at[to], m_to[u], m_self[u], sem))

            @pl.when(relayed[u])
            def _():
                pltpu.make_async_remote_copy(
                    src_ref=out_m.at[at], dst_ref=passed.at[pl.ds(pl.multiple_of(i * tile, tile), tile)], send_sem=send_sem.at[sem],
                    recv_sem=pass_recv.at[i], device_id=middle[u], device_id_type=MESH).start()

    pl.when(edge)(turn)

    def passing(i):
        at = pl.ds(i * tile, tile)
        return pltpu.make_async_remote_copy(
            src_ref=passed.at[at], dst_ref=om_ref.at[at], send_sem=pass_send.at[i], recv_sem=recv_sem.at[m_sem[0]],
            device_id=relay_to, device_id_type=MESH)

    @pl.when(relaying)
    def _():
        for i in range(pieces):
            at = pl.ds(i * tile, tile)
            pltpu.make_async_copy(passed.at[at], passed.at[at], pass_recv.at[i]).wait()
            passing(i).start()
        for i in range(pieces):
            passing(i).wait_send()

    pltpu.make_async_copy(ov_ref, ov_ref, recv_sem.at[v_sem]).wait()
    for u in range(2):
        part = om_ref.at[u * width:(u + 1) * width]
        pltpu.make_async_copy(part, part, recv_sem.at[m_sem[u]]).wait()
    for copy in sends:
        copy.wait_send()
    for far, same, _ in crossed:
        pl.when(jnp.logical_not(same))(far.wait_send)
    v_out = describe(out_v, ov_ref, v_to, v_sem)
    pl.when(jnp.logical_not(v_self))(v_out.wait_send)
    for u in range(2):
        slot = lax.rem(row_to[u], 2)
        sem = jnp.where(slot == 0, m_sem[0], m_sem[1])
        part = out_m.at[u * width:(u + 1) * width]
        out = describe(part, om_ref.at[0:width], m_to[u], sem)
        pl.when(jnp.logical_not(m_self[u]))(out.wait_send)


def settle(*refs):
    given, out, (held, came, left) = refs[:2], refs[2:4], refs[4:]
    parts = came.shape[1]
    rows = given[0].shape[0] // parts
    pieces = [(a, i, slice(i * rows, (i + 1) * rows)) for i in range(parts) for a in range(2)]
    fetch = [pltpu.make_async_copy(given[a].at[at], held.at[a, at], came.at[a, i]) for a, i, at in pieces]
    store = [pltpu.make_async_copy(held.at[a, at], out[a].at[at], left.at[a, i]) for a, i, at in pieces]
    for copy in fetch:
        copy.start()
    for first, second in zip(fetch, store):
        first.wait()
        second.start()
    for copy in store:
        copy.wait()


def solution(mesh):
    n_row, n_col = mesh.shape["row"], mesh.shape["col"]

    def on_device(matrix, vectors, rotations):
        height, width = matrix.shape
        shard = rotations.shape[1]
        any_space = pl.BlockSpec(memory_space=pl.ANY)
        moved = pl.pallas_call(
            functools.partial(kernel, n_row, n_col),
            out_shape=[jax.ShapeDtypeStruct((height, width), F32)] * 2,
            in_specs=[any_space] * 3,
            out_specs=[any_space] * 2,
            scratch_shapes=[
                pltpu.VMEM((height, 2 * width), F32),
                pltpu.VMEM((height, 2 * width), F32),
                pltpu.VMEM((n_col, shard, width), F32),
                pltpu.VMEM((n_col // 4, 2, 2, shard, 2 * width), F32),
                pltpu.VMEM((height, width), BF16),
                pltpu.VMEM((height, width), BF16),
                pltpu.VMEM((height, width), BF16),
                pltpu.VMEM((height, width), BF16),
                pltpu.VMEM((height, width), F32),
                pltpu.VMEM((height, width), F32),
                pltpu.VMEM((width, width), F32),
                pltpu.SemaphoreType.DMA((80,)),
                pltpu.SemaphoreType.DMA((80,)),
                pltpu.SemaphoreType.DMA((3,)),
                pltpu.SemaphoreType.DMA((width // 128,)),
                pltpu.SemaphoreType.DMA((width // 128,)),
            ],
            compiler_params=pltpu.CompilerParams(
                collective_id=0, has_side_effects=True, vmem_limit_bytes=60 * 1024 * 1024),
            name="round",
        )(matrix, vectors, rotations)
        return pl.pallas_call(
            settle,
            out_shape=[jax.ShapeDtypeStruct((height, width), F32)] * 2,
            in_specs=[any_space] * 2,
            out_specs=[any_space] * 2,
            scratch_shapes=[
                pltpu.VMEM((2, height, width), F32),
                pltpu.SemaphoreType.DMA((2, 4)),
                pltpu.SemaphoreType.DMA((2, 4)),
            ],
            compiler_params=pltpu.CompilerParams(vmem_limit_bytes=60 * 1024 * 1024),
            name="settle",
        )(*moved)

    return jax.shard_map(
        on_device, mesh=mesh,
        in_specs=(P("row", "col"), P("row", "col"), P("row", "col", None)),
        out_specs=(P("row", "col"), P("row", "col")), check_vma=False)
```
